32 devices in a mesh: replica: 2 (over x), node: 2 (over core), rank: 8 (over z, y).
Axes of the slice: x: 2, y: 2, z: 4, core: 2. Of those that a mesh axis runs over, the one named last changes fastest.
Arguments:
- hidden_rows: bfloat16 [2048, 3584], P(('replica', 'node', 'rank')), parts along dimension 0, may hold values from -6 to 6
- routes: int32 [2048, 8], P(('replica', 'node', 'rank')), parts along dimension 0, may hold values from 0 to 15, all different within a row; in each aligned block of 64 rows (0 to 63, 64 to 127, ...) at most 48 rows name the same one
- route_weights: float32 [2048, 8], P(('replica', 'node', 'rank')), parts along dimension 0, may hold values from 0.1 to 1
- w_gate: bfloat16 [16, 3584, 1024], P(('node', 'rank')), may hold values from -0.09375 to 0.09375
- w_up: bfloat16 [16, 3584, 1024], P(('node', 'rank')), may hold values from -0.09375 to 0.09375
- w_down: bfloat16 [16, 1024, 3584], P(('node', 'rank')), may hold values from -0.1875 to 0.1875
- queries: bfloat16 [256, 64, 576], P(('replica', 'node', 'rank')), parts along dimension 0, may hold values from -40 to 40
- kv_cache: bfloat16 [256, 256, 576], P(('replica', 'node', 'rank')), parts along dimension 0, may hold values from -5 to 5
- lengths: int32 [256], P(('replica', 'node', 'rank')), parts along dimension 0, may hold values from 2 to 256, as said below
Outputs:
- mixed_rows: bfloat16 [2048, 3584], P(('replica', 'node', 'rank')), parts along dimension 0
- attended: bfloat16 [256, 64, 512], P(('replica', 'node', 'rank')), parts along dimension 0
The draws below stay inside these ranges and needn't reach their ends.
There are 2 independent parts, one for each index of `replica`. The reference program is written for one: setup_inputs(seed, part) draws one part's arguments, and reference() takes and returns one part's arrays. A program takes and returns all parts, laid end to end along the dimension named above; an argument that names none is the same for every part. Nothing has to cross between parts.
Inputs may be any that keep to these rules, and one draw needn't show every extreme that they name: `routes`: each row names 8 different experts; among the 64 rows of one device no expert is named by more than 48 rows, a bound that some block reaches. `lengths`: row 0 has length 256.
All inputs are finite; a program needn't handle non-finite values.
Results may differ from the reference program's by a relative error of at most 0.006.
Values may be sent and summed in bfloat16 or wider, within the bound.
No kernel may reach another device: no remote copies, remote signals or barrier semaphores. Data moves between devices by JAX's collectives and lax.ppermute only.
A program may use at most 128 MiB of HBM per device.

```python
import math
import jax
import jax.numpy as jnp
import numpy as np
from jax import lax

D = 3584
FF = 1024
TOP = 8
TOK_DEV = 64
HEADS = 64
LATENT = 512
CACHE_LEN = 256
EXPERTS = 16
TOKENS = 1024
CAP = 48
KV = 576
B_ROWS = 128
N_NODE = 2
N_RANK = 8


def cache_normal(key):
    return jnp.clip(jax.random.normal(key, (B_ROWS, CACHE_LEN, KV), jnp.float32), -5.0, 5.0)


def draw_kv_cache(key, part):
    base_normal = cache_normal(key)
    return base_normal.astype(jnp.bfloat16)


def draw_queries(key, part):
    own_key = jax.random.fold_in(key, 7)
    noise_draw = jnp.clip(jax.random.normal(own_key, (B_ROWS, HEADS, KV), jnp.float32), -5.0, 5.0)
    return noise_draw.astype(jnp.bfloat16)


def draw_lengths(key, part):
    own_key = jax.random.fold_in(key, 11)
    drawn = jax.random.randint(own_key, (B_ROWS,), 2, CACHE_LEN + 1, jnp.int32)
    row_index = jnp.arange(B_ROWS, dtype=jnp.int32)
    return jnp.where(row_index == 0, CACHE_LEN, drawn).astype(jnp.int32)


def block_scale(key, dims, pieces, least, largest):
    loudness, own = 1.0, jax.random.fold_in(key, 6)
    for position, blocks in pieces:
        draws = jnp.exp(jax.random.uniform(jax.random.fold_in(own, position), (blocks,), jnp.float32, least / len(pieces), largest / len(pieces)))
        loudness = loudness * jnp.repeat(draws, dims[position] // blocks).reshape([-1 if axis == position else 1 for axis in range(len(dims))])
    return loudness


def routed_block(rng, own, number, rows, count, top, reach, slope):
    ranking = jax.random.permutation(rng, count)
    crowded, common = portions_of(count, rows * top, reach, slope, True), portions_of(count, rows * top, reach, slope, False)
    places = jnp.arange(count)

    def named(sizes, rotation):
        used = int((sizes > 0).sum())
        fixed = max(1, used // 4)
        moved = fixed + (places - fixed + rotation * (used - fixed)) % max(1, count - fixed)
        return jnp.zeros((count,), jnp.int32).at[ranking[jnp.where(places < fixed, places, moved)]].set(jnp.asarray(sizes, jnp.int32))

    sizes = jnp.where(number % 4 == 0, named(crowded, number // 4), named(common, number - number // 4 - 1))
    mixed = jax.random.permutation(jax.random.fold_in(own, 3), count)
    source_of, taker = mixed[0:count // 2 * 2:2], mixed[1:count // 2 * 2:2]
    margin = jnp.minimum(sizes[source_of] - 1, reach - sizes[taker]) // 2
    margin = jnp.where((source_of == ranking[0]) | (taker == ranking[0]) | (sizes[taker] == 0), 0, jnp.maximum(margin, 0))
    moved = jax.random.randint(jax.random.fold_in(own, 4), (count // 2,), 0, 1 << 20) % (margin + 1)
    sizes = sizes.at[source_of].add(-moved).at[taker].add(moved)
    members = jnp.searchsorted(jnp.cumsum(sizes), jnp.arange(rows * top), side="right").astype(jnp.int32)
    grid = members.reshape(top, rows).T
    grid = grid[jax.random.permutation(jax.random.fold_in(own, 1), rows)]
    rotation = jax.random.randint(jax.random.fold_in(own, 2), (rows, 1), 0, top)
    return jnp.take_along_axis(grid, (jnp.arange(top)[None, :] + rotation) % top, axis=1)


def portions_of(number_of, total, bound, slope, full):
    weights = [(1 << 20) // math.isqrt(grade ** slope) + 1 for grade in range(1, number_of + 1)]
    largest = bound if full else min(bound, max(-(-total // number_of), total * weights[0] // sum(weights)))
    least = 1 if total - largest >= number_of - 1 else 0
    given, spare = [largest] + [least] * (number_of - 1), total - largest - least * (number_of - 1)
    while spare > 0:
        movable = [i for i in range(1, number_of) if given[i] < largest] or [i for i in range(1, number_of) if given[i] < bound]
        mass, remaining = sum([weights[i] for i in movable]), spare
        for i in movable:
            addition = min(bound - given[i], max(1, remaining * weights[i] // mass), spare)
            given[i] = given[i] + addition
            spare = spare - addition
    return np.array(given)


def centred(rng, extent, scale, limit, split=(), held_as=jnp.bfloat16):
    factor_of = block_scale(rng, extent, split, -0.22, 0.18) if split else 1.0
    values = jax.random.normal(rng, extent, jnp.float32) * scale * factor_of
    return jnp.minimum(jnp.maximum(values, -limit), limit).astype(held_as)


def setup_inputs(seed: int = 0, part: int = 0) -> dict:
    streams_of = jax.random.split(jax.random.key(seed), 10)
    own_keys = jax.random.split(jax.random.fold_in(streams_of[9], part), 10)
    hidden_rows = centred(own_keys[0], (TOKENS, D), 1.0, 6.0, ((0, 16),))
    routes_keys = jax.random.split(jax.random.fold_in(own_keys[1], 1), TOKENS // TOK_DEV)
    routes_turns = jax.random.permutation(jax.random.fold_in(own_keys[1], 3), TOKENS // TOK_DEV)
    routes = jax.vmap(lambda own, number: routed_block(jax.random.fold_in(own_keys[1], 2), own, number, TOK_DEV, EXPERTS, TOP, CAP, 2))(routes_keys, routes_turns).reshape((TOKENS, TOP))
    route_weights = jnp.clip(jnp.exp(math.log(1.0) - 2.3025851 * jax.random.uniform(own_keys[2], (TOKENS, TOP), jnp.float32) ** block_scale(own_keys[2], (TOKENS, TOP), ((0, 16),), -0.2, 0.2)), 0.1, 1.0)
    w_gate = centred(streams_of[3], (EXPERTS, D, FF), D ** -0.5, 0.09375, ((0, 16),))
    w_up = centred(streams_of[4], (EXPERTS, D, FF), D ** -0.5, 0.09375, ((0, 16),))
    w_down = centred(streams_of[5], (EXPERTS, FF, D), FF ** -0.5, 0.1875, ((0, 16),))
    queries = draw_queries(jax.random.fold_in(jax.random.fold_in(streams_of[9], part), 71), part)
    kv_cache = draw_kv_cache(jax.random.fold_in(jax.random.fold_in(streams_of[9], part), 71), part)
    lengths = draw_lengths(jax.random.fold_in(jax.random.fold_in(streams_of[9], part), 71), part)
    return dict(hidden_rows=hidden_rows, routes=routes, route_weights=route_weights, w_gate=w_gate, w_up=w_up, w_down=w_down, queries=queries, kv_cache=kv_cache, lengths=lengths)


score_scale = 192.0 ** -0.5


def expert_rows(gathered, gate_weight, up_weight, down_weight):
    gate_term = jnp.dot(gathered, gate_weight, preferred_element_type=jnp.float32)
    up_term = jnp.dot(gathered, up_weight, preferred_element_type=jnp.float32)
    hidden = (jax.nn.silu(gate_term) * up_term).astype(jnp.bfloat16)
    return jnp.dot(hidden, down_weight, preferred_element_type=jnp.float32).astype(jnp.bfloat16)


def attend_row(query_row, cache_row, length):
    scores = jnp.dot(query_row, cache_row.T, preferred_element_type=jnp.float32) * score_scale
    active = jnp.arange(CACHE_LEN, dtype=jnp.int32) < length
    scores = jnp.where(active[None, :], scores, -jnp.inf)
    row_max = jnp.max(scores, axis=1, keepdims=True)
    exponent = jnp.exp(scores - row_max)
    softmax_weights = (exponent / jnp.sum(exponent, axis=1, keepdims=True)).astype(jnp.bfloat16)
    return jnp.dot(softmax_weights, cache_row[:, :LATENT], preferred_element_type=jnp.float32).astype(jnp.bfloat16)


def reference(hidden_rows, routes, route_weights, w_gate, w_up, w_down, queries, kv_cache, lengths):
    flat_routes = routes.reshape(-1)
    flat_weights = route_weights.reshape(-1)
    slot_count = N_NODE * N_RANK * CAP

    def one_expert(expert_index):
        matches = flat_routes == expert_index
        located = jnp.nonzero(matches, size=slot_count, fill_value=0)[0].astype(jnp.int32)
        active = (jnp.arange(slot_count, dtype=jnp.int32) < jnp.sum(matches.astype(jnp.int32))).astype(jnp.float32)
        owner_rows = (located // TOP).astype(jnp.int32)
        produced = expert_rows(hidden_rows[owner_rows], w_gate[expert_index], w_up[expert_index], w_down[expert_index])
        weighted = produced.astype(jnp.float32) * (flat_weights[located] * active)[:, None]
        return owner_rows, weighted

    owners, weighted = lax.map(one_expert, jnp.arange(EXPERTS, dtype=jnp.int32))
    mixed_rows = jnp.zeros((TOKENS, D), jnp.float32).at[owners.reshape(-1)].add(weighted.reshape(-1, D))
    attended = lax.map(lambda items: attend_row(items[0], items[1], items[2]), (queries, kv_cache, lengths))
    return mixed_rows.astype(jnp.bfloat16), attended
```

```python
import jax
import jax.numpy as jnp
from jax import lax
from jax.experimental import pallas as pl
from jax.experimental.pallas import tpu as pltpu
from jax.sharding import PartitionSpec as P

LATENT = 512
PAIR = 2


score_scale = 192.0 ** (-0.5)


def attend(queries, kv_cache, lengths):
    scores = (
        jnp.einsum("bhc,blc->bhl", queries, kv_cache, preferred_element_type=jnp.float32)
        * score_scale
    )
    visible = lax.broadcasted_iota(jnp.int32, (1, 1, kv_cache.shape[1]), 2) < lengths[:, None, None]
    scores = jnp.where(visible, scores, -jnp.inf)
    row_max = jnp.max(scores, axis=2, keepdims=True)
    exponent = jnp.exp(scores - row_max)
    softmax_weights = (exponent / jnp.sum(exponent, axis=2, keepdims=True)).astype(jnp.bfloat16)
    latent_values = kv_cache[:, :, :LATENT]
    return jnp.einsum(
        "bhl,blc->bhc", softmax_weights, latent_values, preferred_element_type=jnp.float32
    ).astype(jnp.bfloat16)


def expert_kernel(own, other, own_y, other_y, weight, gate, up, down, keep, send, rows, total):
    step = pl.program_id(0)
    tokens = own.shape[0]

    @pl.when(step == 0)
    def _():
        for place, block in enumerate((own, own_y, other, other_y)):
            rows[place * tokens : (place + 1) * tokens, :] = block[...]

    gate_term = jnp.dot(rows[...], gate[0], preferred_element_type=jnp.float32)
    up_term = jnp.dot(rows[...], up[0], preferred_element_type=jnp.float32)
    hidden = (gate_term / (1.0 + jnp.exp(-gate_term)) * up_term).astype(jnp.bfloat16)
    part = jnp.dot(hidden, down[0], preferred_element_type=jnp.float32)

    @pl.when(step == 0)
    def _():
        total[...] = part

    @pl.when(step > 0)
    def _():
        total[...] += part

    @pl.when(step == pl.num_programs(0) - 1)
    def _():
        half = 2 * tokens
        for place, out in enumerate((keep, send)):
            span = slice(place * half, (place + 1) * half)
            produced = total[span, :].astype(jnp.bfloat16).astype(jnp.float32)
            out[...] = (produced * weight[span, :]).astype(jnp.bfloat16)


def run_expert(blocks, weight, w_gate, w_up, w_down):
    tokens, model_width = blocks[0].shape
    hidden_width = w_gate.shape[2]
    tile = 256
    whole = pl.BlockSpec((tokens, model_width), lambda f: (0, 0))
    half = pl.BlockSpec((2 * tokens, model_width), lambda f: (0, 0))
    return pl.pallas_call(
        expert_kernel,
        grid=(hidden_width // tile,),
        out_shape=[jax.ShapeDtypeStruct((2 * tokens, model_width), jnp.bfloat16)] * 2,
        in_specs=[whole] * 4
        + [
            pl.BlockSpec((4 * tokens, 1), lambda f: (0, 0)),
            pl.BlockSpec((1, model_width, tile), lambda f: (0, 0, f)),
            pl.BlockSpec((1, model_width, tile), lambda f: (0, 0, f)),
            pl.BlockSpec((1, tile, model_width), lambda f: (0, f, 0)),
        ],
        out_specs=[half, half],
        scratch_shapes=[
            pltpu.VMEM((4 * tokens, model_width), jnp.bfloat16),
            pltpu.VMEM((4 * tokens, model_width), jnp.float32),
        ],
        compiler_params=pltpu.CompilerParams(vmem_limit_bytes=40 * 1024 * 1024),
        cost_estimate=pl.CostEstimate(
            flops=2 * 3 * 4 * tokens * model_width * hidden_width,
            bytes_accessed=3 * 2 * model_width * hidden_width + 16 * tokens * model_width,
            transcendentals=4 * tokens * hidden_width,
        ),
    )(*blocks, weight, w_gate, w_up, w_down)


def local(hidden_rows, routes, route_weights, w_gate, w_up, w_down, queries, kv_cache, lengths):
    tokens = hidden_rows.shape[0]
    node_count = lax.axis_size("node")
    rank_count = lax.axis_size("rank")
    experts = node_count * rank_count * w_gate.shape[0]
    steps = rank_count // PAIR
    f32, bf16 = jnp.float32, jnp.bfloat16

    def core(value):
        return lax.ppermute(value, "node", [(i, 1 - i) for i in range(node_count)])

    def pair(value):
        return lax.ppermute(value, "rank", [(i, i ^ 1) for i in range(rank_count)])

    def ring(value):
        return lax.ppermute(value, "rank", [(i, (i + PAIR) % rank_count) for i in range(rank_count)])

    chosen = routes[:, :, None] == jnp.arange(experts, dtype=jnp.int32)[None, None, :]
    dense = jnp.sum(jnp.where(chosen, route_weights[:, :, None], 0.0), axis=1)
    mine = lax.all_to_all(
        dense.T.reshape(experts, tokens), ("node", "rank"), split_axis=0, concat_axis=0, tiled=True
    ).reshape(node_count, rank_count, tokens)
    node, rank = lax.axis_index("node"), lax.axis_index("rank")

    def weight_of(slot):
        at = lax.rem(rank // PAIR - slot + steps, steps) * PAIR
        here = lax.rem(rank, PAIR)
        order = [(node, at + here), (node, at + 1 - here), (1 - node, at + here), (1 - node, at + 1 - here)]
        return jnp.concatenate([mine[n, r] for n, r in order])[:, None]

    own = [hidden_rows]
    for _ in range(steps - 1):
        own.append(ring(own[-1]))
    partial = []
    for slot in range(steps):
        own_y = pair(own[slot])
        blocks = (own[slot], core(own[slot]), own_y, core(own_y))
        partial.append(run_expert(blocks, weight_of(slot), w_gate, w_up, w_down))

    attended = attend(queries, kv_cache, lengths)

    def reduced(slot):
        keep, send = partial[slot]
        got = core(send)
        away = (keep[tokens:].astype(f32) + got[tokens:].astype(f32)).astype(bf16)
        back = pair(away)
        return keep[:tokens].astype(f32) + got[:tokens].astype(f32) + back.astype(f32)

    carried = None
    for slot in list(range(1, steps)) + [0]:
        value = reduced(slot)
        if carried is not None:
            value = value + carried.astype(f32)
        value = value.astype(bf16)
        carried = ring(value) if slot else value
    return (carried, attended)


def solution(mesh):
    return jax.shard_map(
        local,
        mesh=mesh,
        in_specs=(
            P(("replica", "node", "rank"), None),
            P(("replica", "node", "rank"), None),
            P(("replica", "node", "rank"), None),
            P(("node", "rank"), None, None),
            P(("node", "rank"), None, None),
            P(("node", "rank"), None, None),
            P(("replica", "node", "rank"), None, None),
            P(("replica", "node", "rank"), None, None),
            P(("replica", "node", "rank")),
        ),
        out_specs=(
            P(("replica", "node", "rank"), None),
            P(("replica", "node", "rank"), None, None),
        ),
        check_vma=False,
    )
```

```python
import jax
import jax.numpy as jnp
from jax import lax
from jax.experimental import pallas as pl
from jax.experimental.pallas import tpu as pltpu
from jax.sharding import PartitionSpec as P

LATENT = 512
PAIR = 2


VMEM_LIMIT = 16 * 1024 * 1024
score_scale = 192.0 ** (-0.5)


def attend(queries, kv_cache, lengths):
    scores = (
        jnp.einsum("bhc,blc->bhl", queries, kv_cache, preferred_element_type=jnp.float32)
        * score_scale
    )
    visible = lax.broadcasted_iota(jnp.int32, (1, 1, kv_cache.shape[1]), 2) < lengths[:, None, None]
    scores = jnp.where(visible, scores, -jnp.inf)
    row_max = jnp.max(scores, axis=2, keepdims=True)
    exponent = jnp.exp(scores - row_max)
    softmax_weights = (exponent / jnp.sum(exponent, axis=2, keepdims=True)).astype(jnp.bfloat16)
    latent_values = kv_cache[:, :, :LATENT]
    return jnp.einsum(
        "bhl,blc->bhc", softmax_weights, latent_values, preferred_element_type=jnp.float32
    ).astype(jnp.bfloat16)


def extend_kernel(experts, hidden, routes, route_weights, out):
    tokens, model_width = hidden.shape
    out[:, :model_width] = hidden[...]
    shape = (tokens, out.shape[1] - model_width)
    lane = lax.broadcasted_iota(jnp.int32, shape, 1)
    group = (lane >= experts).astype(jnp.int32) + (lane >= 2 * experts).astype(jnp.int32)
    expert = lane - group * experts
    weight = jnp.zeros(shape, jnp.float32)
    for k in range(routes.shape[1]):
        weight += jnp.where(routes[:, k : k + 1] == expert, route_weights[:, k : k + 1], 0.0)
    high = weight.astype(jnp.bfloat16).astype(jnp.float32)
    middle = (weight - high).astype(jnp.bfloat16).astype(jnp.float32)
    low = weight - high - middle
    part = jnp.where(group == 0, high, jnp.where(group == 1, middle, low))
    out[:, model_width:] = part.astype(jnp.bfloat16)


def extend(hidden_rows, routes, route_weights, experts):
    tokens, model_width = hidden_rows.shape
    extra = -(-3 * experts // 128) * 128
    inside = pl.BlockSpec(memory_space=pltpu.VMEM)
    return pl.pallas_call(
        lambda *refs: extend_kernel(experts, *refs),
        out_shape=jax.ShapeDtypeStruct((tokens, model_width + extra), jnp.bfloat16),
        in_specs=[inside] * 3,
        out_specs=inside,
        compiler_params=pltpu.CompilerParams(vmem_limit_bytes=VMEM_LIMIT),
        cost_estimate=pl.CostEstimate(flops=0, bytes_accessed=hidden_rows.size * 4, transcendentals=0),
    )(hidden_rows, routes, route_weights)


def expert_kernel(experts, own, other, own_y, other_y, gate, up, down, keep, send, rows):
    tokens = own.shape[0]
    model_width = gate.shape[0]
    for place, block in enumerate((own, own_y, other, other_y)):
        rows[place * tokens : (place + 1) * tokens, :] = block[...]
    extra = rows[:, model_width:].astype(jnp.float32)
    lane = lax.broadcasted_iota(jnp.int32, extra.shape, 1)
    mine = lax.axis_index("node") * lax.axis_size("rank") + lax.axis_index("rank")
    at = (lane == mine) | (lane == mine + experts) | (lane == mine + 2 * experts)
    weight = jnp.sum(jnp.where(at, extra, 0.0), axis=1, keepdims=True)
    values = rows[:, :model_width]
    gate_term = jnp.dot(values, gate[...], preferred_element_type=jnp.float32)
    up_term = jnp.dot(values, up[...], preferred_element_type=jnp.float32)
    hidden = (gate_term / (1.0 + jnp.exp(-gate_term)) * up_term).astype(jnp.bfloat16)
    produced = jnp.dot(hidden, down[...], preferred_element_type=jnp.float32)
    produced = (produced.astype(jnp.bfloat16).astype(jnp.float32) * weight).astype(jnp.bfloat16)
    keep[...] = produced[: 2 * tokens]
    send[...] = produced[2 * tokens :]


def load_kernel(*refs):
    count = len(refs) // 3
    copies = [
        pltpu.make_async_copy(refs[i], refs[count + i], refs[2 * count + i]) for i in range(count)
    ]
    for copy in copies:
        copy.start()
    for copy in copies:
        copy.wait()


def load_inside(*arrays):
    return pl.pallas_call(
        load_kernel,
        out_shape=[jax.ShapeDtypeStruct(a.shape, a.dtype) for a in arrays],
        in_specs=[pl.BlockSpec(memory_space=pl.ANY)] * len(arrays),
        out_specs=[pl.BlockSpec(memory_space=pltpu.VMEM)] * len(arrays),
        scratch_shapes=[pltpu.SemaphoreType.DMA] * len(arrays),
        compiler_params=pltpu.CompilerParams(vmem_limit_bytes=VMEM_LIMIT),
        cost_estimate=pl.CostEstimate(
            flops=0, bytes_accessed=sum(a.size * 2 for a in arrays), transcendentals=0
        ),
    )(*arrays)


def run_expert(experts, blocks, w_gate, w_up, w_down):
    tokens, extended = blocks[0].shape
    model_width, hidden_width = w_gate.shape
    inside = pl.BlockSpec(memory_space=pltpu.VMEM)
    return pl.pallas_call(
        lambda *refs: expert_kernel(experts, *refs),
        out_shape=[jax.ShapeDtypeStruct((2 * tokens, model_width), jnp.bfloat16)] * 2,
        in_specs=[inside] * 7,
        out_specs=[inside] * 2,
        scratch_shapes=[pltpu.VMEM((4 * tokens, extended), jnp.bfloat16)],
        compiler_params=pltpu.CompilerParams(vmem_limit_bytes=VMEM_LIMIT),
        cost_estimate=pl.CostEstimate(
            flops=2 * 3 * 4 * tokens * model_width * hidden_width,
            bytes_accessed=16 * tokens * model_width,
            transcendentals=4 * tokens * hidden_width,
        ),
    )(*blocks, w_gate, w_up, w_down)


def local(hidden_rows, routes, route_weights, w_gate, w_up, w_down, queries, kv_cache, lengths):
    tokens = hidden_rows.shape[0]
    node_count = lax.axis_size("node")
    rank_count = lax.axis_size("rank")
    experts = node_count * rank_count * w_gate.shape[0]
    steps = rank_count // PAIR
    f32, bf16 = jnp.float32, jnp.bfloat16

    def core(value):
        return lax.ppermute(value, "node", [(i, 1 - i) for i in range(node_count)])

    def pair(value):
        return lax.ppermute(value, "rank", [(i, i ^ 1) for i in range(rank_count)])

    def ring(value):
        return lax.ppermute(value, "rank", [(i, (i + PAIR) % rank_count) for i in range(rank_count)])

    weights = load_inside(w_gate[0], w_up[0], w_down[0])

    attended = attend(queries, kv_cache, lengths)

    own = [extend(hidden_rows, routes, route_weights, experts)]
    other, own_y, other_y, partial = [], [], [], []
    for slot in range(steps):
        arrived = {"own_y": pair(own[slot]), "other": core(own[slot])}
        if slot < steps - 1:
            arrived["own"] = ring(own[slot])
        if slot == 0:
            arrived["weights"] = weights
        else:
            other_y.append(core(own_y[slot - 1]))
            blocks = own[slot - 1], other[slot - 1], own_y[slot - 1], other_y[slot - 1]
            arrived["partial"] = run_expert(experts, blocks, *weights)
        arrived = lax.optimization_barrier(arrived)
        own_y.append(arrived["own_y"])
        other.append(arrived["other"])
        if slot < steps - 1:
            own.append(arrived["own"])
        if slot == 0:
            weights = arrived["weights"]
        else:
            partial.append(arrived["partial"])
    other_y.append(core(own_y[-1]))
    blocks = own[-1], other[-1], own_y[-1], other_y[-1]
    partial.append(run_expert(experts, blocks, *weights))

    got = [core(send) for keep, send in partial]

    def away(slot):
        return pair((partial[slot][0][tokens:].astype(f32) + got[slot][tokens:].astype(f32)).astype(bf16))

    def kept(slot):
        return partial[slot][0][:tokens].astype(f32) + got[slot][:tokens].astype(f32)

    back = {}
    carried = None
    for slot in list(range(1, steps)) + [0]:
        back[slot] = away(slot)
        value = kept(slot) + back[slot].astype(f32)
        if carried is not None:
            value = value + carried.astype(f32)
        value = value.astype(bf16)
        carried = ring(value) if slot else value
    return (carried, attended)


def solution(mesh):
    return jax.shard_map(
        local,
        mesh=mesh,
        in_specs=(
            P(("replica", "node", "rank"), None),
            P(("replica", "node", "rank"), None),
            P(("replica", "node", "rank"), None),
            P(("node", "rank"), None, None),
            P(("node", "rank"), None, None),
            P(("node", "rank"), None, None),
            P(("replica", "node", "rank"), None, None),
            P(("replica", "node", "rank"), None, None),
            P(("replica", "node", "rank")),
        ),
        out_specs=(
            P(("replica", "node", "rank"), None),
            P(("replica", "node", "rank"), None, None),
        ),
        check_vma=False,
    )
```

```python
import jax
import jax.numpy as jnp
from jax import lax
from jax.experimental import pallas as pl
from jax.experimental.pallas import tpu as pltpu
from jax.sharding import PartitionSpec as P

LATENT = 512
PAIR = 2


VMEM_LIMIT = 28 * 1024 * 1024
LOAD_LIMIT = 28 * 1024 * 1024
score_scale = 192.0 ** (-0.5)


def attend(queries, kv_cache, lengths):
    scores = (
        jnp.einsum("bhc,blc->bhl", queries, kv_cache, preferred_element_type=jnp.float32)
        * score_scale
    )
    visible = lax.broadcasted_iota(jnp.int32, (1, 1, kv_cache.shape[1]), 2) < lengths[:, None, None]
    scores = jnp.where(visible, scores, -jnp.inf)
    row_max = jnp.max(scores, axis=2, keepdims=True)
    exponent = jnp.exp(scores - row_max)
    softmax_weights = (exponent / jnp.sum(exponent, axis=2, keepdims=True)).astype(jnp.bfloat16)
    latent_values = kv_cache[:, :, :LATENT]
    return jnp.einsum(
        "bhl,blc->bhc", softmax_weights, latent_values, preferred_element_type=jnp.float32
    ).astype(jnp.bfloat16)


def extend_kernel(experts, hidden, routes, route_weights, out, sem):
    tokens, model_width = hidden.shape
    copy = pltpu.make_async_copy(hidden, out.at[:, :model_width], sem)
    copy.start()
    shape = (tokens, out.shape[1] - model_width)
    lane = lax.broadcasted_iota(jnp.int32, shape, 1)
    group = (lane >= experts).astype(jnp.int32) + (lane >= 2 * experts).astype(jnp.int32)
    expert = lane - group * experts
    weight = jnp.zeros(shape, jnp.float32)
    route, route_weight = routes[...].T, route_weights[...].T
    for k in range(routes.shape[0]):
        weight += jnp.where(route[:, k : k + 1] == expert, route_weight[:, k : k + 1], 0.0)
    high = weight.astype(jnp.bfloat16).astype(jnp.float32)
    middle = (weight - high).astype(jnp.bfloat16).astype(jnp.float32)
    low = weight - high - middle
    part = jnp.where(group == 0, high, jnp.where(group == 1, middle, low))
    out[:, model_width:] = part.astype(jnp.bfloat16)
    copy.wait()


def extend(hidden_rows, routes, route_weights, experts):
    tokens, model_width = hidden_rows.shape
    extra = -(-3 * experts // 128) * 128
    inside = pl.BlockSpec(memory_space=pltpu.VMEM)
    return pl.pallas_call(
        lambda *refs: extend_kernel(experts, *refs),
        out_shape=jax.ShapeDtypeStruct((tokens, model_width + extra), jnp.bfloat16),
        in_specs=[pl.BlockSpec(memory_space=pl.ANY), inside, inside],
        out_specs=inside,
        scratch_shapes=[pltpu.SemaphoreType.DMA],
        compiler_params=pltpu.CompilerParams(vmem_limit_bytes=60 * 1024 * 1024),
        cost_estimate=pl.CostEstimate(flops=0, bytes_accessed=hidden_rows.size * 4, transcendentals=0),
    )(hidden_rows, routes.T, route_weights.T)


def expert_kernel(experts, own, other, own_y, other_y, gate, up, down, *refs):
    outs, rows = refs[:-1], refs[-1]
    tokens = own.shape[0]
    model_width = gate.shape[0]
    for place, block in enumerate((own, own_y, other, other_y)):
        rows[place * tokens : (place + 1) * tokens, :] = block[...]
    extra = rows[:, model_width:].astype(jnp.float32)
    lane = lax.broadcasted_iota(jnp.int32, extra.shape, 1)
    mine = lax.axis_index("node") * lax.axis_size("rank") + lax.axis_index("rank")
    at = (lane == mine) | (lane == mine + experts) | (lane == mine + 2 * experts)
    weight = jnp.sum(jnp.where(at, extra, 0.0), axis=1, keepdims=True)
    values = rows[:, :model_width]
    gate_term = jnp.dot(values, gate[...], preferred_element_type=jnp.float32)
    up_term = jnp.dot(values, up[...], preferred_element_type=jnp.float32)
    hidden = (gate_term / (1.0 + jnp.exp(-gate_term)) * up_term).astype(jnp.bfloat16)
    produced = jnp.dot(hidden, down[...], preferred_element_type=jnp.float32)
    produced = (produced.astype(jnp.bfloat16).astype(jnp.float32) * weight).astype(jnp.bfloat16)
    for place, out in enumerate(outs):
        out[...] = produced[place * tokens : (place + 1) * tokens]


def load_kernel(*refs):
    count = len(refs) // 3
    copies = [
        pltpu.make_async_copy(refs[i], refs[count + i], refs[2 * count + i]) for i in range(count)
    ]
    for copy in copies:
        copy.start()
    for copy in copies:
        copy.wait()


def load_inside(*arrays):
    return pl.pallas_call(
        load_kernel,
        out_shape=[jax.ShapeDtypeStruct(a.shape, a.dtype) for a in arrays],
        in_specs=[pl.BlockSpec(memory_space=pl.ANY)] * len(arrays),
        out_specs=[pl.BlockSpec(memory_space=pltpu.VMEM)] * len(arrays),
        scratch_shapes=[pltpu.SemaphoreType.DMA] * len(arrays),
        compiler_params=pltpu.CompilerParams(vmem_limit_bytes=LOAD_LIMIT),
        cost_estimate=pl.CostEstimate(
            flops=0, bytes_accessed=sum(a.size * 2 for a in arrays), transcendentals=0
        ),
    )(*arrays)


def run_expert(experts, blocks, w_gate, w_up, w_down):
    tokens, extended = blocks[0].shape
    model_width, hidden_width = w_gate.shape
    inside = pl.BlockSpec(memory_space=pltpu.VMEM)
    return pl.pallas_call(
        lambda *refs: expert_kernel(experts, *refs),
        out_shape=[jax.ShapeDtypeStruct((tokens, model_width), jnp.bfloat16)] * 4,
        in_specs=[inside] * 7,
        out_specs=[inside] * 4,
        scratch_shapes=[pltpu.VMEM((4 * tokens, extended), jnp.bfloat16)],
        compiler_params=pltpu.CompilerParams(vmem_limit_bytes=VMEM_LIMIT),
        cost_estimate=pl.CostEstimate(flops=0, bytes_accessed=0, transcendentals=0),
    )(*blocks, w_gate, w_up, w_down)


def local(hidden_rows, routes, route_weights, w_gate, w_up, w_down, queries, kv_cache, lengths):
    tokens = hidden_rows.shape[0]
    node_count = lax.axis_size("node")
    rank_count = lax.axis_size("rank")
    experts = node_count * rank_count * w_gate.shape[0]
    steps = rank_count // PAIR
    f32, bf16 = jnp.float32, jnp.bfloat16

    def core(value):
        return lax.ppermute(value, "node", [(i, 1 - i) for i in range(node_count)])

    def pair(value):
        return lax.ppermute(value, "rank", [(i, i ^ 1) for i in range(rank_count)])

    def ring(value):
        return lax.ppermute(value, "rank", [(i, (i + PAIR) % rank_count) for i in range(rank_count)])

    weights = load_inside(w_gate[0], w_up[0], w_down[0])

    own, own_y, other, other_y = [extend(hidden_rows, routes, route_weights, experts)], [], [], []
    keep, keep_y, got, got_y, back = [], [], [], [], {}

    def compute(slot):
        other_y.append(core(own_y[slot]))
        blocks = own[slot], other[slot], own_y[slot], other_y[slot]
        kept, kept_y, sent, sent_y = run_expert(experts, blocks, *weights)
        keep.append(kept)
        keep_y.append(kept_y)
        got_y.append(core(sent_y))
        got.append(core(sent))

    def away(slot):
        return pair((keep_y[slot].astype(f32) + got_y[slot].astype(f32)).astype(bf16))

    def onward(slot, carried):
        value = keep[slot].astype(f32) + got[slot].astype(f32) + back[slot].astype(f32)
        if carried is not None:
            value = value + carried.astype(f32)
        return value.astype(bf16)

    for slot in range(steps):
        arrived = {"other": core(own[slot])}
        if slot < steps - 1 or steps < 3:
            arrived["own_y"] = pair(own[slot])
        else:
            arrived["own_y"] = ring(own_y[slot - 1])
            arrived["back"] = away(1)
        if slot < steps - 1:
            arrived["own"] = ring(own[slot])
        if slot == 0:
            arrived["weights"] = weights
        else:
            compute(slot - 1)
            arrived["keep"] = keep_y[slot - 1]
        arrived = lax.optimization_barrier(arrived)
        other.append(arrived["other"])
        own_y.append(arrived["own_y"])
        if "own" in arrived:
            own.append(arrived["own"])
        if "weights" in arrived:
            weights = arrived["weights"]
        if "keep" in arrived:
            keep_y[slot - 1] = arrived["keep"]
        if "back" in arrived:
            back[1] = arrived["back"]

    attended = attend(queries, kv_cache, lengths)

    order = list(range(1, steps)) + [0]
    if steps > 1 and 1 not in back:
        back[1] = away(1)
    carried = None
    for place, slot in enumerate(order[:-1]):
        arrived = {"carried": ring(onward(slot, carried))}
        if place == 0:
            compute(steps - 1)
            arrived["keep"] = keep_y[-1]
        following = order[place + 1]
        arrived["back"] = away(following)
        arrived = lax.optimization_barrier(arrived)
        carried, back[following] = arrived["carried"], arrived["back"]
        if place == 0:
            keep_y[-1] = arrived["keep"]
    return (onward(0, carried), attended)


def solution(mesh):
    return jax.shard_map(
        local,
        mesh=mesh,
        in_specs=(
            P(("replica", "node", "rank"), None),
            P(("replica", "node", "rank"), None),
            P(("replica", "node", "rank"), None),
            P(("node", "rank"), None, None),
            P(("node", "rank"), None, None),
            P(("node", "rank"), None, None),
            P(("replica", "node", "rank"), None, None),
            P(("replica", "node", "rank"), None, None),
            P(("replica", "node", "rank")),
        ),
        out_specs=(
            P(("replica", "node", "rank"), None),
            P(("replica", "node", "rank"), None, None),
        ),
        check_vma=False,
    )
```

```python
import jax
import jax.numpy as jnp
from jax import lax
from jax.experimental import pallas as pl
from jax.experimental.pallas import tpu as pltpu
from jax.sharding import PartitionSpec as P

LATENT = 512
PAIR = 2


VMEM_LIMIT = 28 * 1024 * 1024
LOAD_LIMIT = 28 * 1024 * 1024
score_scale = 192.0 ** (-0.5)


def attend(queries, kv_cache, lengths):
    scores = (
        jnp.einsum("bhc,blc->bhl", queries, kv_cache, preferred_element_type=jnp.float32)
        * score_scale
    )
    visible = lax.broadcasted_iota(jnp.int32, (1, 1, kv_cache.shape[1]), 2) < lengths[:, None, None]
    scores = jnp.where(visible, scores, -jnp.inf)
    row_max = jnp.max(scores, axis=2, keepdims=True)
    exponent = jnp.exp(scores - row_max)
    softmax_weights = (exponent / jnp.sum(exponent, axis=2, keepdims=True)).astype(jnp.bfloat16)
    latent_values = kv_cache[:, :, :LATENT]
    return jnp.einsum(
        "bhl,blc->bhc", softmax_weights, latent_values, preferred_element_type=jnp.float32
    ).astype(jnp.bfloat16)


def extend_kernel(experts, hidden, routes, route_weights, out, sem):
    tokens, model_width = hidden.shape
    copy = pltpu.make_async_copy(hidden, out.at[:, :model_width], sem)
    copy.start()
    shape = (tokens, out.shape[1] - model_width)
    lane = lax.broadcasted_iota(jnp.int32, shape, 1)
    group = (lane >= experts).astype(jnp.int32) + (lane >= 2 * experts).astype(jnp.int32)
    expert = lane - group * experts
    weight = jnp.zeros(shape, jnp.float32)
    route, route_weight = routes[...].T, route_weights[...].T
    for k in range(routes.shape[0]):
        weight += jnp.where(route[:, k : k + 1] == expert, route_weight[:, k : k + 1], 0.0)
    high = weight.astype(jnp.bfloat16).astype(jnp.float32)
    middle = (weight - high).astype(jnp.bfloat16).astype(jnp.float32)
    low = weight - high - middle
    part = jnp.where(group == 0, high, jnp.where(group == 1, middle, low))
    out[:, model_width:] = part.astype(jnp.bfloat16)
    copy.wait()


def extend(hidden_rows, routes, route_weights, experts):
    tokens, model_width = hidden_rows.shape
    extra = -(-3 * experts // 128) * 128
    inside = pl.BlockSpec(memory_space=pltpu.VMEM)
    return pl.pallas_call(
        lambda *refs: extend_kernel(experts, *refs),
        out_shape=jax.ShapeDtypeStruct((tokens, model_width + extra), jnp.bfloat16),
        in_specs=[pl.BlockSpec(memory_space=pl.ANY), inside, inside],
        out_specs=inside,
        scratch_shapes=[pltpu.SemaphoreType.DMA],
        compiler_params=pltpu.CompilerParams(vmem_limit_bytes=60 * 1024 * 1024),
        cost_estimate=pl.CostEstimate(flops=0, bytes_accessed=hidden_rows.size * 4, transcendentals=0),
    )(hidden_rows, routes.T, route_weights.T)


def expert_kernel(experts, own, other, own_y, other_y, gate, up, down, *refs):
    outs, rows = refs[:-1], refs[-1]
    tokens = own.shape[0]
    model_width = gate.shape[0]
    for place, block in enumerate((own, own_y, other, other_y)):
        rows[place * tokens : (place + 1) * tokens, :] = block[...]
    extra = rows[:, model_width:].astype(jnp.float32)
    lane = lax.broadcasted_iota(jnp.int32, extra.shape, 1)
    mine = lax.axis_index("node") * lax.axis_size("rank") + lax.axis_index("rank")
    at = (lane == mine) | (lane == mine + experts) | (lane == mine + 2 * experts)
    weight = jnp.sum(jnp.where(at, extra, 0.0), axis=1, keepdims=True)
    values = rows[:, :model_width]
    gate_term = jnp.dot(values, gate[...], preferred_element_type=jnp.float32)
    up_term = jnp.dot(values, up[...], preferred_element_type=jnp.float32)
    hidden = (gate_term / (1.0 + jnp.exp(-gate_term)) * up_term).astype(jnp.bfloat16)
    produced = jnp.dot(hidden, down[...], preferred_element_type=jnp.float32)
    produced = (produced.astype(jnp.bfloat16).astype(jnp.float32) * weight).astype(jnp.bfloat16)
    for place, out in enumerate(outs):
        out[...] = produced[place * tokens : (place + 1) * tokens]


def load_kernel(*refs):
    count = len(refs) // 3
    copies = [
        pltpu.make_async_copy(refs[i], refs[count + i], refs[2 * count + i]) for i in range(count)
    ]
    for copy in copies:
        copy.start()
    for copy in copies:
        copy.wait()


def load_inside(*arrays):
    return pl.pallas_call(
        load_kernel,
        out_shape=[jax.ShapeDtypeStruct(a.shape, a.dtype) for a in arrays],
        in_specs=[pl.BlockSpec(memory_space=pl.ANY)] * len(arrays),
        out_specs=[pl.BlockSpec(memory_space=pltpu.VMEM)] * len(arrays),
        scratch_shapes=[pltpu.SemaphoreType.DMA] * len(arrays),
        compiler_params=pltpu.CompilerParams(vmem_limit_bytes=LOAD_LIMIT),
        cost_estimate=pl.CostEstimate(
            flops=0, bytes_accessed=sum(a.size * 2 for a in arrays), transcendentals=0
        ),
    )(*arrays)


def run_expert(experts, blocks, w_gate, w_up, w_down):
    tokens, extended = blocks[0].shape
    model_width, hidden_width = w_gate.shape
    inside = pl.BlockSpec(memory_space=pltpu.VMEM)
    return pl.pallas_call(
        lambda *refs: expert_kernel(experts, *refs),
        out_shape=[jax.ShapeDtypeStruct((tokens, model_width), jnp.bfloat16)] * 4,
        in_specs=[inside] * 7,
        out_specs=[inside] * 4,
        scratch_shapes=[pltpu.VMEM((4 * tokens, extended), jnp.bfloat16)],
        compiler_params=pltpu.CompilerParams(vmem_limit_bytes=VMEM_LIMIT),
        cost_estimate=pl.CostEstimate(flops=0, bytes_accessed=0, transcendentals=0),
    )(*blocks, w_gate, w_up, w_down)


def local(hidden_rows, routes, route_weights, w_gate, w_up, w_down, queries, kv_cache, lengths):
    tokens = hidden_rows.shape[0]
    node_count = lax.axis_size("node")
    rank_count = lax.axis_size("rank")
    experts = node_count * rank_count * w_gate.shape[0]
    steps = rank_count // PAIR
    f32, bf16 = jnp.float32, jnp.bfloat16

    line = list(range(0, steps, 2)) + list(range(1, steps, 2))[::-1]
    hops = [
        (line[i] * PAIR + j, line[(i + 1) % steps] * PAIR + j) for i in range(steps) for j in range(PAIR)
    ]

    def core(value):
        return lax.ppermute(value, "node", [(i, 1 - i) for i in range(node_count)])

    def pair(value):
        return lax.ppermute(value, "rank", [(i, i ^ 1) for i in range(rank_count)])

    def ring(value):
        return lax.ppermute(value, "rank", hops)

    weights = load_inside(w_gate[0], w_up[0], w_down[0])

    own, own_y, other, other_y = [extend(hidden_rows, routes, route_weights, experts)], [], [], []
    keep, keep_y, got, got_y, back = [], [], [], [], {}

    def compute(slot):
        other_y.append(core(own_y[slot]))
        blocks = own[slot], other[slot], own_y[slot], other_y[slot]
        kept, kept_y, sent, sent_y = run_expert(experts, blocks, *weights)
        keep.append(kept)
        keep_y.append(kept_y)
        got_y.append(core(sent_y))
        got.append(core(sent))

    def away(slot):
        return pair((keep_y[slot].astype(f32) + got_y[slot].astype(f32)).astype(bf16))

    def onward(slot, carried):
        value = keep[slot].astype(f32) + got[slot].astype(f32) + back[slot].astype(f32)
        if carried is not None:
            value = value + carried.astype(f32)
        return value.astype(bf16)

    for slot in range(steps):
        arrived = {"other": core(own[slot])}
        if slot < steps - 1 or steps < 3:
            arrived["own_y"] = pair(own[slot])
        else:
            arrived["own_y"] = ring(own_y[slot - 1])
            arrived["back"] = away(1)
        if slot < steps - 1:
            arrived["own"] = ring(own[slot])
        if slot == 0:
            arrived["weights"] = weights
        else:
            compute(slot - 1)
            arrived["keep"] = keep_y[slot - 1]
        arrived = lax.optimization_barrier(arrived)
        other.append(arrived["other"])
        own_y.append(arrived["own_y"])
        if "own" in arrived:
            own.append(arrived["own"])
        if "weights" in arrived:
            weights = arrived["weights"]
        if "keep" in arrived:
            keep_y[slot - 1] = arrived["keep"]
        if "back" in arrived:
            back[1] = arrived["back"]

    attended = attend(queries, kv_cache, lengths)

    order = list(range(1, steps)) + [0]
    if steps > 1 and 1 not in back:
        back[1] = away(1)
    carried = None
    for place, slot in enumerate(order[:-1]):
        arrived = {"carried": ring(onward(slot, carried))}
        if place == 0:
            compute(steps - 1)
            arrived["keep"] = keep_y[-1]
        following = order[place + 1]
        arrived["back"] = away(following)
        arrived = lax.optimization_barrier(arrived)
        carried, back[following] = arrived["carried"], arrived["back"]
        if place == 0:
            keep_y[-1] = arrived["keep"]
    return (onward(0, carried), attended)


def solution(mesh):
    return jax.shard_map(
        local,
        mesh=mesh,
        in_specs=(
            P(("replica", "node", "rank"), None),
            P(("replica", "node", "rank"), None),
            P(("replica", "node", "rank"), None),
            P(("node", "rank"), None, None),
            P(("node", "rank"), None, None),
            P(("node", "rank"), None, None),
            P(("replica", "node", "rank"), None, None),
            P(("replica", "node", "rank"), None, None),
            P(("replica", "node", "rank")),
        ),
        out_specs=(
            P(("replica", "node", "rank"), None),
            P(("replica", "node", "rank"), None, None),
        ),
        check_vma=False,
    )
```

```python
import jax
import jax.numpy as jnp
from jax import lax
from jax.experimental import pallas as pl
from jax.experimental.pallas import tpu as pltpu
from jax.sharding import PartitionSpec as P

LATENT = 512
PAIR = 2


VMEM_LIMIT = 28 * 1024 * 1024
LOAD_LIMIT = 28 * 1024 * 1024
score_scale = 192.0 ** (-0.5)


def attend(queries, kv_cache, lengths):
    scores = (
        jnp.einsum("bhc,blc->bhl", queries, kv_cache, preferred_element_type=jnp.float32)
        * score_scale
    )
    visible = lax.broadcasted_iota(jnp.int32, (1, 1, kv_cache.shape[1]), 2) < lengths[:, None, None]
    scores = jnp.where(visible, scores, -jnp.inf)
    row_max = jnp.max(scores, axis=2, keepdims=True)
    exponent = jnp.exp(scores - row_max)
    softmax_weights = (exponent / jnp.sum(exponent, axis=2, keepdims=True)).astype(jnp.bfloat16)
    latent_values = kv_cache[:, :, :LATENT]
    return jnp.einsum(
        "bhl,blc->bhc", softmax_weights, latent_values, preferred_element_type=jnp.float32
    ).astype(jnp.bfloat16)


def extend_kernel(experts, hidden, routes, route_weights, out, sem):
    tokens, model_width = hidden.shape
    copy = pltpu.make_async_copy(hidden, out.at[:, :model_width], sem)
    copy.start()
    shape = (tokens, out.shape[1] - model_width)
    lane = lax.broadcasted_iota(jnp.int32, shape, 1)
    group = (lane >= experts).astype(jnp.int32) + (lane >= 2 * experts).astype(jnp.int32)
    expert = lane - group * experts
    weight = jnp.zeros(shape, jnp.float32)
    route, route_weight = routes[...].T, route_weights[...].T
    for k in range(routes.shape[0]):
        weight += jnp.where(route[:, k : k + 1] == expert, route_weight[:, k : k + 1], 0.0)
    high = weight.astype(jnp.bfloat16).astype(jnp.float32)
    middle = (weight - high).astype(jnp.bfloat16).astype(jnp.float32)
    low = weight - high - middle
    part = jnp.where(group == 0, high, jnp.where(group == 1, middle, low))
    out[:, model_width:] = part.astype(jnp.bfloat16)
    copy.wait()


def extend(hidden_rows, routes, route_weights, experts):
    tokens, model_width = hidden_rows.shape
    extra = -(-3 * experts // 128) * 128
    inside = pl.BlockSpec(memory_space=pltpu.VMEM)
    return pl.pallas_call(
        lambda *refs: extend_kernel(experts, *refs),
        out_shape=jax.ShapeDtypeStruct((tokens, model_width + extra), jnp.bfloat16),
        in_specs=[pl.BlockSpec(memory_space=pl.ANY), inside, inside],
        out_specs=inside,
        scratch_shapes=[pltpu.SemaphoreType.DMA],
        compiler_params=pltpu.CompilerParams(vmem_limit_bytes=60 * 1024 * 1024),
        cost_estimate=pl.CostEstimate(flops=0, bytes_accessed=hidden_rows.size * 4, transcendentals=0),
    )(hidden_rows, routes.T, route_weights.T)


def expert_kernel(experts, own, other, own_y, other_y, gate, up, down, *refs):
    outs, rows = refs[:-1], refs[-1]
    tokens = own.shape[0]
    model_width = gate.shape[0]
    for place, block in enumerate((own, own_y, other, other_y)):
        rows[place * tokens : (place + 1) * tokens, :] = block[...]
    extra = rows[:, model_width:].astype(jnp.float32)
    lane = lax.broadcasted_iota(jnp.int32, extra.shape, 1)
    mine = lax.axis_index("node") * lax.axis_size("rank") + lax.axis_index("rank")
    at = (lane == mine) | (lane == mine + experts) | (lane == mine + 2 * experts)
    weight = jnp.sum(jnp.where(at, extra, 0.0), axis=1, keepdims=True)
    values = rows[:, :model_width]
    gate_term = jnp.dot(values, gate[...], preferred_element_type=jnp.float32)
    up_term = jnp.dot(values, up[...], preferred_element_type=jnp.float32)
    hidden = (gate_term / (1.0 + jnp.exp(-gate_term)) * up_term).astype(jnp.bfloat16)
    produced = jnp.dot(hidden, down[...], preferred_element_type=jnp.float32)
    produced = (produced.astype(jnp.bfloat16).astype(jnp.float32) * weight).astype(jnp.bfloat16)
    for place, out in enumerate(outs):
        out[...] = produced[place * tokens : (place + 1) * tokens]


def load_kernel(*refs):
    count = len(refs) // 3
    copies = [
        pltpu.make_async_copy(refs[i], refs[count + i], refs[2 * count + i]) for i in range(count)
    ]
    for copy in copies:
        copy.start()
    for copy in copies:
        copy.wait()


def load_inside(*arrays):
    return pl.pallas_call(
        load_kernel,
        out_shape=[jax.ShapeDtypeStruct(a.shape, a.dtype) for a in arrays],
        in_specs=[pl.BlockSpec(memory_space=pl.ANY)] * len(arrays),
        out_specs=[pl.BlockSpec(memory_space=pltpu.VMEM)] * len(arrays),
        scratch_shapes=[pltpu.SemaphoreType.DMA] * len(arrays),
        compiler_params=pltpu.CompilerParams(vmem_limit_bytes=LOAD_LIMIT),
        cost_estimate=pl.CostEstimate(
            flops=0, bytes_accessed=sum(a.size * 2 for a in arrays), transcendentals=0
        ),
    )(*arrays)


def run_expert(experts, blocks, w_gate, w_up, w_down):
    tokens, extended = blocks[0].shape
    model_width, hidden_width = w_gate.shape
    inside = pl.BlockSpec(memory_space=pltpu.VMEM)
    return pl.pallas_call(
        lambda *refs: expert_kernel(experts, *refs),
        out_shape=[jax.ShapeDtypeStruct((tokens, model_width), jnp.bfloat16)] * 4,
        in_specs=[inside] * 7,
        out_specs=[inside] * 4,
        scratch_shapes=[pltpu.VMEM((4 * tokens, extended), jnp.bfloat16)],
        compiler_params=pltpu.CompilerParams(vmem_limit_bytes=VMEM_LIMIT),
        cost_estimate=pl.CostEstimate(flops=0, bytes_accessed=0, transcendentals=0),
    )(*blocks, w_gate, w_up, w_down)


def add_kernel(*refs):
    terms, out = refs[:-1], refs[-1]
    total = terms[0][...].astype(jnp.float32)
    for term in terms[1:]:
        total += term[...].astype(jnp.float32)
    out[...] = total.astype(jnp.bfloat16)


def add(*terms):
    inside = pl.BlockSpec(memory_space=pltpu.VMEM)
    return pl.pallas_call(
        add_kernel,
        out_shape=jax.ShapeDtypeStruct(terms[0].shape, jnp.bfloat16),
        in_specs=[inside] * len(terms),
        out_specs=inside,
        compiler_params=pltpu.CompilerParams(vmem_limit_bytes=4 * 1024 * 1024),
        cost_estimate=pl.CostEstimate(flops=0, bytes_accessed=0, transcendentals=0),
    )(*terms)


def local(hidden_rows, routes, route_weights, w_gate, w_up, w_down, queries, kv_cache, lengths):
    tokens = hidden_rows.shape[0]
    node_count = lax.axis_size("node")
    rank_count = lax.axis_size("rank")
    experts = node_count * rank_count * w_gate.shape[0]
    steps = rank_count // PAIR
    f32, bf16 = jnp.float32, jnp.bfloat16

    line = list(range(0, steps, 2)) + list(range(1, steps, 2))[::-1]
    hops = [
        (line[i] * PAIR + j, line[(i + 1) % steps] * PAIR + j) for i in range(steps) for j in range(PAIR)
    ]

    def core(value):
        return lax.ppermute(value, "node", [(i, 1 - i) for i in range(node_count)])

    def pair(value):
        return lax.ppermute(value, "rank", [(i, i ^ 1) for i in range(rank_count)])

    def ring(value):
        return lax.ppermute(value, "rank", hops)

    weights = load_inside(w_gate[0], w_up[0], w_down[0])

    own, own_y, other, other_y = [extend(hidden_rows, routes, route_weights, experts)], [], [], []
    keep, keep_y, got, got_y, back = [], [], [], [], {}

    def compute(slot):
        other_y.append(core(own_y[slot]))
        blocks = own[slot], other[slot], own_y[slot], other_y[slot]
        kept, kept_y, sent, sent_y = run_expert(experts, blocks, *weights)
        keep.append(kept)
        keep_y.append(kept_y)
        got_y.append(core(sent_y))
        got.append(core(sent))

    def away(slot):
        return pair((keep_y[slot].astype(f32) + got_y[slot].astype(f32)).astype(bf16))

    def onward(slot, carried):
        terms = [keep[slot], got[slot], back[slot]]
        return add(*terms) if carried is None else add(*terms, carried)

    for slot in range(steps):
        arrived = {"other": core(own[slot])}
        if slot < steps - 1 or steps < 3:
            arrived["own_y"] = pair(own[slot])
        else:
            arrived["own_y"] = ring(own_y[slot - 1])
            arrived["back"] = away(1)
        if slot < steps - 1:
            arrived["own"] = ring(own[slot])
        if slot == 0:
            arrived["weights"] = weights
        else:
            compute(slot - 1)
            arrived["keep"] = keep_y[slot - 1]
        arrived = lax.optimization_barrier(arrived)
        other.append(arrived["other"])
        own_y.append(arrived["own_y"])
        if "own" in arrived:
            own.append(arrived["own"])
        if "weights" in arrived:
            weights = arrived["weights"]
        if "keep" in arrived:
            keep_y[slot - 1] = arrived["keep"]
        if "back" in arrived:
            back[1] = arrived["back"]

    attended = attend(queries, kv_cache, lengths)

    order = list(range(1, steps)) + [0]
    if steps > 1 and 1 not in back:
        back[1] = away(1)
    carried = None
    for place, slot in enumerate(order[:-1]):
        arrived = {"carried": ring(onward(slot, carried))}
        if place == 0:
            compute(steps - 1)
            arrived["keep"] = keep_y[-1]
        following = order[place + 1]
        arrived["back"] = away(following)
        arrived = lax.optimization_barrier(arrived)
        carried, back[following] = arrived["carried"], arrived["back"]
        if place == 0:
            keep_y[-1] = arrived["keep"]
    return (onward(0, carried), attended)


def solution(mesh):
    return jax.shard_map(
        local,
        mesh=mesh,
        in_specs=(
            P(("replica", "node", "rank"), None),
            P(("replica", "node", "rank"), None),
            P(("replica", "node", "rank"), None),
            P(("node", "rank"), None, None),
            P(("node", "rank"), None, None),
            P(("node", "rank"), None, None),
            P(("replica", "node", "rank"), None, None),
            P(("replica", "node", "rank"), None, None),
            P(("replica", "node", "rank")),
        ),
        out_specs=(
            P(("replica", "node", "rank"), None),
            P(("replica", "node", "rank"), None, None),
        ),
        check_vma=False,
    )
```

```python
import jax
import jax.numpy as jnp
from jax import lax
from jax.experimental import pallas as pl
from jax.experimental.pallas import tpu as pltpu
from jax.sharding import PartitionSpec as P

LATENT = 512
PAIR = 2


VMEM_LIMIT = 28 * 1024 * 1024
LOAD_LIMIT = 28 * 1024 * 1024
score_scale = 192.0 ** (-0.5)


def attend(queries, kv_cache, lengths):
    scores = (
        jnp.einsum("bhc,blc->bhl", queries, kv_cache, preferred_element_type=jnp.float32)
        * score_scale
    )
    visible = lax.broadcasted_iota(jnp.int32, (1, 1, kv_cache.shape[1]), 2) < lengths[:, None, None]
    scores = jnp.where(visible, scores, -jnp.inf)
    row_max = jnp.max(scores, axis=2, keepdims=True)
    exponent = jnp.exp(scores - row_max)
    softmax_weights = (exponent / jnp.sum(exponent, axis=2, keepdims=True)).astype(jnp.bfloat16)
    latent_values = kv_cache[:, :, :LATENT]
    return jnp.einsum(
        "bhl,blc->bhc", softmax_weights, latent_values, preferred_element_type=jnp.float32
    ).astype(jnp.bfloat16)


def extend_kernel(experts, hidden, routes, route_weights, out, sem):
    tokens, model_width = hidden.shape
    copy = pltpu.make_async_copy(hidden, out.at[:, :model_width], sem)
    copy.start()
    shape = (tokens, out.shape[1] - model_width)
    lane = lax.broadcasted_iota(jnp.int32, shape, 1)
    group = (lane >= experts).astype(jnp.int32) + (lane >= 2 * experts).astype(jnp.int32)
    expert = lane - group * experts
    weight = jnp.zeros(shape, jnp.float32)
    route, route_weight = routes[...].T, route_weights[...].T
    for k in range(routes.shape[0]):
        weight += jnp.where(route[:, k : k + 1] == expert, route_weight[:, k : k + 1], 0.0)
    high = weight.astype(jnp.bfloat16).astype(jnp.float32)
    middle = (weight - high).astype(jnp.bfloat16).astype(jnp.float32)
    low = weight - high - middle
    part = jnp.where(group == 0, high, jnp.where(group == 1, middle, low))
    out[:, model_width:] = part.astype(jnp.bfloat16)
    copy.wait()


def extend(hidden_rows, routes, route_weights, experts):
    tokens, model_width = hidden_rows.shape
    extra = -(-3 * experts // 128) * 128
    inside = pl.BlockSpec(memory_space=pltpu.VMEM)
    return pl.pallas_call(
        lambda *refs: extend_kernel(experts, *refs),
        out_shape=jax.ShapeDtypeStruct((tokens, model_width + extra), jnp.bfloat16),
        in_specs=[pl.BlockSpec(memory_space=pl.ANY), inside, inside],
        out_specs=inside,
        scratch_shapes=[pltpu.SemaphoreType.DMA],
        compiler_params=pltpu.CompilerParams(vmem_limit_bytes=60 * 1024 * 1024),
        cost_estimate=pl.CostEstimate(flops=0, bytes_accessed=hidden_rows.size * 4, transcendentals=0),
    )(hidden_rows, routes.T, route_weights.T)


def expert_kernel(experts, own, other, own_y, other_y, gate, up, down, *refs):
    outs, rows = refs[:-1], refs[-1]
    tokens = own.shape[0]
    model_width = gate.shape[0]
    for place, block in enumerate((own, own_y, other, other_y)):
        rows[place * tokens : (place + 1) * tokens, :] = block[...]
    extra = rows[:, model_width:].astype(jnp.float32)
    lane = lax.broadcasted_iota(jnp.int32, extra.shape, 1)
    mine = lax.axis_index("node") * lax.axis_size("rank") + lax.axis_index("rank")
    at = (lane == mine) | (lane == mine + experts) | (lane == mine + 2 * experts)
    weight = jnp.sum(jnp.where(at, extra, 0.0), axis=1, keepdims=True)
    values = rows[:, :model_width]
    gate_term = jnp.dot(values, gate[...], preferred_element_type=jnp.float32)
    up_term = jnp.dot(values, up[...], preferred_element_type=jnp.float32)
    hidden = (gate_term / (1.0 + jnp.exp(-gate_term)) * up_term).astype(jnp.bfloat16)
    produced = jnp.dot(hidden, down[...], preferred_element_type=jnp.float32)
    produced = (produced.astype(jnp.bfloat16).astype(jnp.float32) * weight).astype(jnp.bfloat16)
    for place, out in enumerate(outs):
        out[...] = produced[place * tokens : (place + 1) * tokens]


def load_kernel(*refs):
    count = len(refs) // 3
    copies = [
        pltpu.make_async_copy(refs[i], refs[count + i], refs[2 * count + i]) for i in range(count)
    ]
    for copy in copies:
        copy.start()
    for copy in copies:
        copy.wait()


def load_inside(*arrays):
    return pl.pallas_call(
        load_kernel,
        out_shape=[jax.ShapeDtypeStruct(a.shape, a.dtype) for a in arrays],
        in_specs=[pl.BlockSpec(memory_space=pl.ANY)] * len(arrays),
        out_specs=[pl.BlockSpec(memory_space=pltpu.VMEM)] * len(arrays),
        scratch_shapes=[pltpu.SemaphoreType.DMA] * len(arrays),
        compiler_params=pltpu.CompilerParams(vmem_limit_bytes=LOAD_LIMIT),
        cost_estimate=pl.CostEstimate(
            flops=0, bytes_accessed=sum(a.size * 2 for a in arrays), transcendentals=0
        ),
    )(*arrays)


def run_expert(experts, blocks, w_gate, w_up, w_down):
    tokens, extended = blocks[0].shape
    model_width, hidden_width = w_gate.shape
    inside = pl.BlockSpec(memory_space=pltpu.VMEM)
    return pl.pallas_call(
        lambda *refs: expert_kernel(experts, *refs),
        out_shape=[jax.ShapeDtypeStruct((tokens, model_width), jnp.bfloat16)] * 4,
        in_specs=[inside] * 7,
        out_specs=[inside] * 4,
        scratch_shapes=[pltpu.VMEM((4 * tokens, extended), jnp.bfloat16)],
        compiler_params=pltpu.CompilerParams(vmem_limit_bytes=VMEM_LIMIT),
        cost_estimate=pl.CostEstimate(flops=0, bytes_accessed=0, transcendentals=0),
    )(*blocks, w_gate, w_up, w_down)


def add_kernel(*refs):
    terms, out = refs[:-1], refs[-1]
    total = terms[0][...].astype(jnp.float32)
    for term in terms[1:]:
        total += term[...].astype(jnp.float32)
    out[...] = total.astype(jnp.bfloat16)


def add(*terms):
    inside = pl.BlockSpec(memory_space=pltpu.VMEM)
    return pl.pallas_call(
        add_kernel,
        out_shape=jax.ShapeDtypeStruct(terms[0].shape, jnp.bfloat16),
        in_specs=[inside] * len(terms),
        out_specs=inside,
        compiler_params=pltpu.CompilerParams(vmem_limit_bytes=4 * 1024 * 1024),
        cost_estimate=pl.CostEstimate(flops=0, bytes_accessed=0, transcendentals=0),
    )(*terms)


def local(hidden_rows, routes, route_weights, w_gate, w_up, w_down, queries, kv_cache, lengths):
    tokens = hidden_rows.shape[0]
    node_count = lax.axis_size("node")
    rank_count = lax.axis_size("rank")
    experts = node_count * rank_count * w_gate.shape[0]
    steps = rank_count // PAIR

    line = list(range(0, steps, 2)) + list(range(1, steps, 2))[::-1]
    hops = [
        (line[i] * PAIR + j, line[(i + 1) % steps] * PAIR + j) for i in range(steps) for j in range(PAIR)
    ]

    def core(value):
        return lax.ppermute(value, "node", [(i, 1 - i) for i in range(node_count)])

    def pair(value):
        return lax.ppermute(value, "rank", [(i, i ^ 1) for i in range(rank_count)])

    def ring(value):
        return lax.ppermute(value, "rank", hops)

    weights = load_inside(w_gate[0], w_up[0], w_down[0])

    own, own_y, other, other_y = [extend(hidden_rows, routes, route_weights, experts)], [], [], []
    keep, keep_y, got, got_y, back = [], [], [], [], {}

    def compute(slot):
        other_y.append(core(own_y[slot]))
        blocks = own[slot], other[slot], own_y[slot], other_y[slot]
        kept, kept_y, sent, sent_y = run_expert(experts, blocks, *weights)
        keep.append(kept)
        keep_y.append(kept_y)
        got_y.append(core(sent_y))
        got.append(core(sent))

    def away(slot):
        return pair(add(keep_y[slot], got_y[slot]))

    def onward(slot, carried):
        terms = [keep[slot], got[slot], back[slot]]
        return add(*terms) if carried is None else add(*terms, carried)

    for slot in range(steps):
        arrived = {"other": core(own[slot])}
        if slot < steps - 1 or steps < 3:
            arrived["own_y"] = pair(own[slot])
        else:
            arrived["own_y"] = ring(own_y[slot - 1])
            arrived["back"] = away(1)
        if slot < steps - 1:
            arrived["own"] = ring(own[slot])
        if slot == 0:
            arrived["weights"] = weights
        else:
            compute(slot - 1)
            arrived["keep"] = keep_y[slot - 1]
        arrived = lax.optimization_barrier(arrived)
        other.append(arrived["other"])
        own_y.append(arrived["own_y"])
        if "own" in arrived:
            own.append(arrived["own"])
        if "weights" in arrived:
            weights = arrived["weights"]
        if "keep" in arrived:
            keep_y[slot - 1] = arrived["keep"]
        if "back" in arrived:
            back[1] = arrived["back"]

    attended = attend(queries, kv_cache, lengths)

    order = list(range(1, steps)) + [0]
    if steps > 1 and 1 not in back:
        back[1] = away(1)
    carried = None
    for place, slot in enumerate(order[:-1]):
        arrived = {"carried": ring(onward(slot, carried))}
        if place == 0:
            compute(steps - 1)
            arrived["keep"] = keep_y[-1]
        following = order[place + 1]
        arrived["back"] = away(following)
        arrived = lax.optimization_barrier(arrived)
        carried, back[following] = arrived["carried"], arrived["back"]
        if place == 0:
            keep_y[-1] = arrived["keep"]
    return (onward(0, carried), attended)


def solution(mesh):
    return jax.shard_map(
        local,
        mesh=mesh,
        in_specs=(
            P(("replica", "node", "rank"), None),
            P(("replica", "node", "rank"), None),
            P(("replica", "node", "rank"), None),
            P(("node", "rank"), None, None),
            P(("node", "rank"), None, None),
            P(("node", "rank"), None, None),
            P(("replica", "node", "rank"), None, None),
            P(("replica", "node", "rank"), None, None),
            P(("replica", "node", "rank")),
        ),
        out_specs=(
            P(("replica", "node", "rank"), None),
            P(("replica", "node", "rank"), None, None),
        ),
        check_vma=False,
    )
```
